512 devices in a mesh: dp: 8 (over y_lo, core), expert: 64 (over y_hi, z, x).
Axes of the slice: x: 4, y: 8 (y_hi: 2, y_lo: 4; y = y_hi * 4 + y_lo), z: 8, core: 2. Of those that a mesh axis runs over, the one named last changes fastest.
Arguments:
- grad_partial: bfloat16 [8, 3, 3, 8, 192, 5120], P('dp', None, None, None, 'expert'), may hold values from -4 to 4
- params: bfloat16 [3, 3, 1536, 5120], P(None, None, ('dp', 'expert')), may hold values from -0.078125 to 0.078125
- first_moment: float32 [3, 3, 1536, 5120], P(None, None, ('dp', 'expert')), may hold values from -1.5 to 1.5
- second_moment: float32 [3, 3, 1536, 5120], P(None, None, ('dp', 'expert')), may hold values from 0.2 to 2
- tokens: bfloat16 [2, 256, 5120], P(None, 'dp'), may hold values from -6 to 6
- expert_ids: int32 [2, 256, 2], P(None, 'dp'), may hold values from 0 to 2, all different within a row
- route_weights: float32 [2, 256, 2], P(None, 'dp'), may hold values from 0.2 to 1
Outputs:
- mixed: bfloat16 [2, 256, 5120], P(None, 'dp')
The draws below stay inside these ranges and needn't reach their ends.
Inputs may be any that keep to these rules, and one draw needn't show every extreme that they name: `expert_ids`: each token names 2 different experts.
All inputs are finite; a program needn't handle non-finite values.
Results may differ from the reference program's by a relative error of at most 0.018.
Values may be sent and summed in bfloat16 or wider, within the bound.
A program may use at most 64 MiB of HBM per device.

```python
import math
import jax
import jax.numpy as jnp
from jax import lax

D = 5120
H = 1536
EXPERTS = 3
TOPK = 2
STEPS = 2
TOKENS = 256
N_DP = 8


def levels(rng, extent, pieces, least, high):
    factor_of = 1.0
    for dim, shards_of in pieces:
        draws = jax.random.uniform(jax.random.fold_in(jax.random.fold_in(rng, 6), dim), (shards_of,), jnp.float32, least / len(pieces), high / len(pieces))
        factor_of = factor_of * jnp.repeat(jnp.exp(draws), extent[dim] // shards_of).reshape((-1,) + (1,) * (len(extent) - 1 - dim))
    return factor_of


def distinct(rng, rows, count, top, lift):
    ranking = jax.random.permutation(jax.random.fold_in(rng, 1), count)
    boost = ranking
    for power in range(3):
        boost = boost * boost // count
    boost = boost * lift // count
    chance = jax.random.randint(jax.random.fold_in(rng, 2), (rows, count), 0, 4096) + boost
    sure = jax.random.permutation(jax.random.fold_in(rng, 3), rows)[jnp.arange(count) % rows]
    chance = jnp.where(jnp.arange(rows)[:, None] == sure[None, :], 1 << 14, chance)
    merit = chance * count + jnp.arange(count)
    return lax.top_k(merit.astype(jnp.int32), top)[1].astype(jnp.int32)


def scatter_about(own_key, dims, deviation, reach, split=(), kind=jnp.bfloat16):
    result = jax.random.normal(own_key, dims, jnp.float32) * deviation
    if len(split) > 0:
        result = levels(own_key, dims, split, -0.22, 0.18) * result
    return jnp.clip(result, min=-reach, max=reach).astype(kind)


def setup_inputs(seed: int = 0) -> dict:
    keys = jax.random.split(jax.random.key(seed), 8)
    grad_partial = scatter_about(keys[0], (N_DP, EXPERTS, 3, N_DP, H // N_DP, D), 0.25, 4.0, ((0, 8), (4, 64)))
    params = scatter_about(keys[1], (EXPERTS, 3, H, D), D ** -0.5, 0.078125, ((2, 512),))
    first_moment = scatter_about(keys[2], (EXPERTS, 3, H, D), 0.1, 1.5, ((2, 512),), jnp.float32)
    second_moment = jnp.clip(jnp.exp(math.log(2.0) - 2.3025851 * jax.random.uniform(keys[3], (EXPERTS, 3, H, D), jnp.float32) ** levels(keys[3], (EXPERTS, 3, H, D), ((2, 512),), -0.2, 0.2)), 0.2, 2.0)
    tokens = scatter_about(keys[4], (STEPS, TOKENS, D), 1.0, 6.0, ((1, 8),))
    expert_ids = distinct(keys[5], STEPS * TOKENS, EXPERTS, TOPK, 0).reshape((STEPS, TOKENS, TOPK))
    route_weights = jnp.clip(0.2 + 0.8 * jax.random.uniform(keys[6], (STEPS, TOKENS, TOPK), jnp.float32) ** levels(keys[6], (STEPS, TOKENS, TOPK), ((1, 8),), -0.2, 0.2), 0.2, 1.0)
    return dict(grad_partial=grad_partial, params=params, first_moment=first_moment, second_moment=second_moment, tokens=tokens, expert_ids=expert_ids, route_weights=route_weights)


def reference(grad_partial, params, first_moment, second_moment, tokens, expert_ids, route_weights):

    def add_one(index, total):
        return total + grad_partial[index].astype(jnp.float32).reshape(params.shape)
    grad = lax.fori_loop(0, N_DP, add_one, jnp.zeros(params.shape, jnp.float32))
    moment_one = 0.9 * first_moment + 0.1 * grad
    moment_two = 0.95 * second_moment + 0.05 * grad * grad
    weights = params.astype(jnp.float32)
    rate = 3.0 / D ** 0.5
    step_dir = moment_one / (1.0 - 0.9 ** 10) / (jnp.sqrt(moment_two / (1.0 - 0.95 ** 10)) + 1e-08)
    new_weights = (weights - rate * (step_dir + 0.1 * weights)).astype(jnp.bfloat16)
    chosen = (expert_ids[..., None] == jnp.arange(EXPERTS, dtype=jnp.int32)).astype(jnp.float32)
    combine = lax.optimization_barrier(jnp.sum(route_weights[..., None] * chosen, axis=-2))
    wide = new_weights.astype(jnp.float32)
    flat = tokens.astype(jnp.float32)
    gate = jnp.einsum('std,xhd->stxh', flat, wide[:, 0])
    up = jnp.einsum('std,xhd->stxh', flat, wide[:, 1])
    hidden = (combine[..., None] * jax.nn.silu(gate) * up).astype(jnp.bfloat16)
    mixed = jnp.einsum('stxh,xhd->std', hidden.astype(jnp.float32), wide[:, 2])
    return mixed.astype(jnp.bfloat16)
```

```python
import functools

import jax
import jax.numpy as jnp
from jax import lax
from jax.experimental import pallas as pl
from jax.experimental.pallas import tpu as pltpu
from jax.sharding import PartitionSpec as P

D = 5120
NX = 4
NZ = 8
ROWS = 16
WIDE = 1024
PARTS = D // WIDE
MESH = pl.DeviceIdType.MESH


def greet(peers):
    barrier = pltpu.get_barrier_semaphore()
    for peer in peers:
        pl.semaphore_signal(barrier, inc=1, device_id=peer, device_id_type=MESH)
    pl.semaphore_wait(barrier, len(peers))


def remote(src, dst, send, recv, peer):
    return pltpu.make_async_remote_copy(
        src_ref=src, dst_ref=dst, send_sem=send, recv_sem=recv, device_id=peer, device_id_type=MESH
    )


def expect(ref, sem):
    pltpu.make_async_copy(ref, ref, sem).wait()


def reduce_kernel(part_ref, out_ref, sx, rx, sz, rz, sy, ry, res, send, recv):
    dp = lax.axis_index("dp")
    e = lax.axis_index("expert")
    half = e // (NX * NZ)
    z = (e // NX) % NZ
    x = e % NX
    x_peer = [(dp, half * NX * NZ + z * NX + (x + d) % NX) for d in range(1, NX)]
    z_peer = [(dp, half * NX * NZ + ((z + d) % NZ) * NX + x) for d in range(1, NZ)]
    y_peer = (dp, (1 - half) * NX * NZ + z * NX + x)
    greet(x_peer + z_peer + [y_peer])

    def lanes(q):
        return pl.ds(pl.multiple_of(q * WIDE, WIDE), WIDE)

    def x_out(q):
        for d in range(1, NX):
            to = (x + d) % NX
            rows = pl.ds(pl.multiple_of(to * ROWS, ROWS), ROWS)
            sx[q, d - 1] = part_ref[rows, lanes(q)].astype(jnp.bfloat16)
            remote(sx.at[q, d - 1], rx.at[q, d - 1], send.at[0, q], recv.at[0, q], x_peer[d - 1]).start()

    def z_out(q):
        expect(rx.at[q], recv.at[0, q])
        rows = pl.ds(pl.multiple_of(x * ROWS, ROWS), ROWS)
        total = part_ref[rows, lanes(q)]
        for d in range(1, NX):
            total += rx[q, d - 1].astype(jnp.float32)
        total = total.astype(jnp.bfloat16)
        for k in range(NZ):
            sz[q, k] = total[:, k * 128 : (k + 1) * 128]
        for d in range(1, NZ):
            to = (z + d) % NZ
            remote(sz.at[q, to], rz.at[q, d - 1], send.at[1, q], recv.at[1, q], z_peer[d - 1]).start()

    def y_out(q):
        expect(rz.at[q], recv.at[1, q])
        total = sz[q, z].astype(jnp.float32)
        for d in range(1, NZ):
            total += rz[q, d - 1].astype(jnp.float32)
        sy[q] = total.astype(jnp.bfloat16)
        remote(sy.at[q], ry.at[q], send.at[2, q], recv.at[2, q], y_peer).start()

    def z_back(q):
        expect(ry.at[q], recv.at[2, q])
        total = sy[q].astype(jnp.float32) + ry[q].astype(jnp.float32)
        res[q, x, z] = total.astype(jnp.bfloat16)
        for d in range(1, NZ):
            remote(res.at[q, x, z], res.at[q, x, z], send.at[3, q], recv.at[3, q], z_peer[d - 1]).start()

    def x_back(q):
        expect(rz.at[q], recv.at[3, q])
        for d in range(1, NX):
            remote(res.at[q, x], res.at[q, x], send.at[4, q], recv.at[4, q], x_peer[d - 1]).start()

    def finish(q):
        expect(rx.at[q], recv.at[4, q])
        for i in range(NX):
            for k in range(NZ):
                columns = pl.ds(pl.multiple_of(q * WIDE + k * 128, 128), 128)
                out_ref[i * ROWS : (i + 1) * ROWS, columns] = res[q, i, k]
        expect(sx.at[q], send.at[0, q])
        expect(rz.at[q], send.at[1, q])
        expect(sy.at[q], send.at[2, q])
        expect(rz.at[q], send.at[3, q])
        expect(rx.at[q], send.at[4, q])

    stages = (x_out, z_out, y_out, z_back, x_back, finish)

    def turn(i, carry):
        for lag, stage in enumerate(stages):
            q = i - lag

            @pl.when((q >= 0) & (q < PARTS))
            def _():
                stage(q)

        return carry

    lax.fori_loop(0, PARTS + len(stages) - 1, turn, 0)


def reduce_out(part):
    tokens = part.shape[0]
    return pl.pallas_call(
        reduce_kernel,
        out_shape=jax.ShapeDtypeStruct((tokens, D), jnp.bfloat16),
        in_specs=[pl.BlockSpec(memory_space=pltpu.VMEM)],
        out_specs=pl.BlockSpec(memory_space=pltpu.VMEM),
        scratch_shapes=[
            pltpu.VMEM((PARTS, NX - 1, ROWS, WIDE), jnp.bfloat16),
            pltpu.VMEM((PARTS, NX - 1, ROWS, WIDE), jnp.bfloat16),
            pltpu.VMEM((PARTS, NZ, ROWS, 128), jnp.bfloat16),
            pltpu.VMEM((PARTS, NZ - 1, ROWS, 128), jnp.bfloat16),
            pltpu.VMEM((PARTS, ROWS, 128), jnp.bfloat16),
            pltpu.VMEM((PARTS, ROWS, 128), jnp.bfloat16),
            pltpu.VMEM((PARTS, NX, NZ, ROWS, 128), jnp.bfloat16),
            pltpu.SemaphoreType.DMA((5, PARTS)),
            pltpu.SemaphoreType.DMA((5, PARTS)),
        ],
        compiler_params=pltpu.CompilerParams(
            collective_id=0, has_side_effects=True, vmem_limit_bytes=40 * 2**20
        ),
    )(part)


def expert_rows(flat, combine, rows):
    projected = jnp.einsum("td,xmhd->txmh", flat, rows[:, :2], preferred_element_type=jnp.float32)
    gate = projected[:, :, 0]
    up = projected[:, :, 1]
    hidden = (combine[..., None] * jax.nn.silu(gate) * up).astype(jnp.bfloat16)
    return jnp.einsum("txh,xhd->td", hidden, rows[:, 2], preferred_element_type=jnp.float32)


def shards(grad_partial, params, first_moment, second_moment, tokens, expert_ids, route_weights):
    summed = lax.psum_scatter(grad_partial, "dp", scatter_dimension=3, tiled=True).astype(
        jnp.float32
    )
    grad = summed.reshape(params.shape)
    moment_one = 0.9 * first_moment + 0.1 * grad
    moment_two = 0.95 * second_moment + 0.05 * grad * grad
    weights = params.astype(jnp.float32)
    rate = 3.0 / D**0.5
    step_dir = moment_one / (1.0 - 0.9**10) / (jnp.sqrt(moment_two / (1.0 - 0.95**10)) + 1e-08)
    new_weights = (weights - rate * (step_dir + 0.1 * weights)).astype(jnp.bfloat16)
    num_steps, num_tok, width = tokens.shape
    num_experts = new_weights.shape[0]
    flat = tokens.reshape(num_steps * num_tok, width)
    chosen = (expert_ids[..., None] == jnp.arange(num_experts, dtype=jnp.int32)).astype(jnp.float32)
    combine = jnp.sum(route_weights[..., None] * chosen, axis=-2).reshape(
        num_steps * num_tok, num_experts
    )
    rollout = lax.all_gather(new_weights, "dp", axis=2, tiled=True)
    partial_out = expert_rows(flat, combine, rollout)
    mixed = reduce_out(partial_out)
    return mixed.reshape(num_steps, num_tok, width)


def solution(mesh):
    return jax.shard_map(
        shards,
        mesh=mesh,
        in_specs=(
            P("dp", None, None, None, "expert", None),
            P(None, None, ("dp", "expert"), None),
            P(None, None, ("dp", "expert"), None),
            P(None, None, ("dp", "expert"), None),
            P(None, "dp", None),
            P(None, "dp", None),
            P(None, "dp", None),
        ),
        out_specs=P(None, "dp", None),
        check_vma=False,
    )
```

```python
import jax
import jax.numpy as jnp
from jax import lax
from jax.experimental import pallas as pl
from jax.experimental.pallas import tpu as pltpu
from jax.sharding import PartitionSpec as P

D = 5120
EXPERTS = 3
HELD = 3
NY = 4
NX = 4
NZ = 8
ROWS = 16
WIDE = 1024
FOLD = WIDE // 128
PARTS = D // WIDE
UNITS = 3 * PARTS
TILES = EXPERTS * HELD
TOKENS = 64
HIDDEN = TILES * 8
RATE = 3.0 / D**0.5
MESH = pl.DeviceIdType.MESH
BF = jnp.bfloat16
F32 = jnp.float32


def remote(src, dst, send, recv, peer):
    return pltpu.make_async_remote_copy(
        src_ref=src, dst_ref=dst, send_sem=send, recv_sem=recv, device_id=peer, device_id_type=MESH
    )


def expect(ref, sem):
    pltpu.make_async_copy(ref, ref, sem).wait()


def kernel(
    grad_hbm,
    par_hbm,
    one_hbm,
    two_hbm,
    tok_hbm,
    comb_ref,
    out_ref,
    gbuf,
    par,
    one,
    two,
    tok,
    fold,
    near,
    right,
    left,
    made,
    flat,
    opt,
    tot,
    wide,
    acc,
    hid,
    part,
    sx,
    rx,
    sz,
    rz,
    sy,
    ry,
    res,
    load_sem,
    in_sem,
    near_send,
    near_recv,
    line_send,
    right_recv,
    left_recv,
    made_send,
    made_recv,
    share_send,
    share_recv,
    send,
    recv,
):
    dp = lax.axis_index("dp")
    e = lax.axis_index("expert")
    y = dp // 2
    c = dp % 2
    half = e // (NX * NZ)
    z = (e // NX) % NZ
    x = e % NX
    x_peer = [(dp, half * NX * NZ + z * NX + (x + d) % NX) for d in range(1, NX)]
    z_peer = [(dp, half * NX * NZ + ((z + d) % NZ) * NX + x) for d in range(1, NZ)]
    far = (dp, (1 - half) * NX * NZ + z * NX + x)
    twin = (y * 2 + 1 - c, e)
    has_up = y < NY - 1
    has_down = y > 0
    edge = ((y == 0) | (y == NY - 1)).astype(jnp.int32)

    up = (((y + 1) % NY) * 2 + c, e)
    down = (((y + NY - 1) % NY) * 2 + c, e)
    peers = x_peer + z_peer + [far, twin, up, down]
    barrier = pltpu.get_barrier_semaphore()
    for peer in peers:
        pl.semaphore_signal(barrier, inc=1, device_id=peer, device_id_type=MESH)

    def lanes(q):
        return pl.ds(pl.multiple_of(q * WIDE, WIDE), WIDE)

    def load(k):
        return pltpu.make_async_copy(
            grad_hbm.at[:, k // PARTS, :, :, lanes(k % PARTS)], gbuf.at[k], load_sem.at[k]
        )

    inputs = [
        pltpu.make_async_copy(a, b, in_sem.at[i])
        for i, (a, b) in enumerate(((par_hbm, par), (one_hbm, one), (two_hbm, two), (tok_hbm, tok)))
    ]

    def start_load(k, carry):
        load(k).start()
        return carry

    lax.fori_loop(0, UNITS, start_load, 0)
    for copy in inputs:
        copy.start()
    acc[...] = jnp.zeros_like(acc)
    pl.semaphore_wait(barrier, len(peers))
    for copy in inputs:
        copy.wait()

    def split(k):
        load(k).wait()
        for t in range(TILES):
            v = gbuf[k, t // HELD, t % HELD].astype(F32)
            for s in range(FOLD):
                flat[pl.ds(t * 64 + s, 8, stride=8), :] = v[:, s * 128 : (s + 1) * 128]
        for t in range(TILES):
            for b in range(8):
                fold[k, (b % 2) * NY + b // 2, t] = flat[t * 64 + b * 8 : t * 64 + b * 8 + 8, :].astype(BF)
        remote(
            fold.at[k, pl.ds((1 - c) * NY, NY)], near.at[k], near_send.at[k], near_recv.at[k], twin
        ).start()

    def send_up(k, to):
        remote(
            fold.at[k, c * NY + to], right.at[k, to], line_send.at[k], right_recv.at[k, to], up
        ).start()

    def send_down(k, to):
        remote(
            fold.at[k, c * NY + to], left.at[k, to], line_send.at[k], left_recv.at[k, to], down
        ).start()

    def pair(k):
        expect(near.at[k], near_recv.at[k])
        for i in range(NY):
            to = jnp.where(y < 2, NY - 1 - i, i)
            mine = c * NY + to
            fold[k, mine] = (fold[k, mine].astype(F32) + near[k, to].astype(F32)).astype(BF)

            @pl.when((y == 0) & (to > 0))
            def _():
                send_up(k, to)

            @pl.when((y == NY - 1) & (to < NY - 1))
            def _():
                send_down(k, to)

    def pass_up(k):
        for to in (3, 2):

            @pl.when(to > y)
            def _():
                expect(right.at[k, to], right_recv.at[k, to])
                mine = c * NY + to
                fold[k, mine] = (fold[k, mine].astype(F32) + right[k, to].astype(F32)).astype(BF)
                send_up(k, to)

    def pass_down(k):
        for to in (0, 1):

            @pl.when(to < y)
            def _():
                expect(left.at[k, to], left_recv.at[k, to])
                mine = c * NY + to
                fold[k, mine] = (fold[k, mine].astype(F32) + left[k, to].astype(F32)).astype(BF)
                send_down(k, to)

    def share(k, of):
        remote(
            made.at[k, of * 2 + c], made.at[k, of * 2 + c], share_send.at[k], share_recv.at[k], twin
        ).start()

    def give_up(k, of):
        remote(
            made.at[k, of * 2 + c], made.at[k, of * 2 + c], made_send.at[k], made_recv.at[k, of], up
        ).start()

    def give_down(k, of):
        remote(
            made.at[k, of * 2 + c], made.at[k, of * 2 + c], made_send.at[k], made_recv.at[k, of], down
        ).start()

    def update(k):
        m = k // PARTS
        q = k % PARTS
        for g in range(EXPERTS):
            for i, source in enumerate((par, one, two)):
                v = source[g, m, :, lanes(q)].astype(F32)
                for s in range(FOLD):
                    opt[i, pl.ds(g * HELD * 8 + s, HELD, stride=8), :] = v[:, s * 128 : (s + 1) * 128]
        tot[...] = fold[k, c * NY + y].astype(F32)

        @pl.when(has_down)
        def _():
            expect(right.at[k, y], right_recv.at[k, y])
            tot[...] += right[k, y].astype(F32)

        @pl.when(has_up)
        def _():
            expect(left.at[k, y], left_recv.at[k, y])
            tot[...] += left[k, y].astype(F32)

        grad = tot[...].reshape(TILES * 8, 128)
        weights = opt[0]
        moment_one = 0.9 * opt[1] + 0.1 * grad
        moment_two = 0.95 * opt[2] + 0.05 * grad * grad
        step_dir = moment_one / (1.0 - 0.9**10) / (jnp.sqrt(moment_two / (1.0 - 0.95**10)) + 1e-08)
        fresh = weights - RATE * (step_dir + 0.1 * weights)
        made[k, dp] = fresh.reshape(TILES, 8, 128).astype(BF)

        @pl.when(has_up)
        def _():
            give_up(k, y)

        @pl.when(has_down)
        def _():
            give_down(k, y)

        share(k, y)

    def gather(k, of):
        expect(made.at[k, of * 2 + c], made_recv.at[k, of])

        @pl.when((of < y) & has_up)
        def _():
            give_up(k, of)

        @pl.when((of > y) & has_down)
        def _():
            give_down(k, of)

        share(k, of)

    def apply(k):
        m = k // PARTS
        q = k % PARTS
        expect(near.at[k], share_recv.at[k])
        for t in range(TILES):
            for b in range(8):
                flat[t * 64 + b * 8 : t * 64 + b * 8 + 8, :] = made[k, b, t].astype(F32)
        for s in range(FOLD):
            rows = [flat[pl.ds(t * 64 + s, 8, stride=8), :] for t in range(TILES)]
            wide[:, s * 128 : (s + 1) * 128] = jnp.concatenate(rows, axis=0).astype(BF)

        @pl.when(m < 2)
        def _():
            acc[m] += lax.dot_general(
                tok[:, lanes(q)], wide[...], (((1,), (1,)), ((), ())), preferred_element_type=F32
            )

        @pl.when(k == 2 * PARTS - 1)
        def _():
            gate = acc[0]
            hid[...] = (comb_ref[...] * (gate / (1.0 + jnp.exp(-gate))) * acc[1]).astype(BF)

        @pl.when(m == 2)
        def _():
            part[q] = jnp.dot(hid[...], wide[...], preferred_element_type=F32)
            for d in range(1, NX):
                to = (x + d) % NX
                rows = pl.ds(pl.multiple_of(to * ROWS, ROWS), ROWS)
                sx[q, d - 1] = part[q, rows, :].astype(BF)
                remote(sx.at[q, d - 1], rx.at[q, d - 1], send.at[0, q], recv.at[0, q], x_peer[d - 1]).start()

    def z_out(q):
        expect(rx.at[q], recv.at[0, q])
        rows = pl.ds(pl.multiple_of(x * ROWS, ROWS), ROWS)
        total = part[q, rows, :]
        for d in range(1, NX):
            total += rx[q, d - 1].astype(F32)
        total = total.astype(BF)
        for k in range(NZ):
            sz[q, k] = total[:, k * 128 : (k + 1) * 128]
        for d in range(1, NZ):
            to = (z + d) % NZ
            remote(sz.at[q, to], rz.at[q, d - 1], send.at[1, q], recv.at[1, q], z_peer[d - 1]).start()

    def y_out(q):
        expect(rz.at[q], recv.at[1, q])
        total = sz[q, z].astype(F32)
        for d in range(1, NZ):
            total += rz[q, d - 1].astype(F32)
        sy[q] = total.astype(BF)
        remote(sy.at[q], ry.at[q], send.at[2, q], recv.at[2, q], far).start()

    def z_back(q):
        expect(ry.at[q], recv.at[2, q])
        total = sy[q].astype(F32) + ry[q].astype(F32)
        res[q, x, z] = total.astype(BF)
        for d in range(1, NZ):
            remote(res.at[q, x, z], res.at[q, x, z], send.at[3, q], recv.at[3, q], z_peer[d - 1]).start()

    def x_back(q):
        expect(rz.at[q], recv.at[3, q])
        for d in range(1, NX):
            remote(res.at[q, x], res.at[q, x], send.at[4, q], recv.at[4, q], x_peer[d - 1]).start()

    def finish(q):
        expect(rx.at[q], recv.at[4, q])
        for i in range(NX):
            for k in range(NZ):
                columns = pl.ds(pl.multiple_of(q * WIDE + k * 128, 128), 128)
                out_ref[i * ROWS : (i + 1) * ROWS, columns] = res[q, i, k]

    def turn(i, carry):
        def at(lag, stage, also=None, first=0):
            k = i - lag
            ok = (k >= first) & (k < UNITS)
            if also is not None:
                ok = ok & also

            @pl.when(ok)
            def _():
                stage(k)

        middle = edge == 0
        at(0, split)
        at(1, pair)
        at(1 + y, pass_up, middle)
        at(4 - y, pass_down, middle)
        at(3 + edge, update)
        for far_off in range(1, NY):
            for of, there in ((y - far_off, y >= far_off), (y + far_off, y + far_off < NY)):
                made_at = 3 + ((of == 0) | (of == NY - 1)).astype(jnp.int32)
                at(made_at + far_off, lambda k, of=of: gather(k, of), there)
        done = 7 + edge
        at(done, apply)
        for lag, stage in enumerate((z_out, y_out, z_back, x_back, finish)):
            at(done + 1 + lag, lambda k, stage=stage: stage(k - 2 * PARTS), None, 2 * PARTS)
        return carry

    lax.fori_loop(0, UNITS + 13, turn, 0)

    def drain(k, carry):
        expect(near.at[k], near_send.at[k])
        expect(near.at[k, 0:3], line_send.at[k])
        expect(near.at[k], share_send.at[k])

        @pl.when(edge == 1)
        def _():
            expect(made.at[k, 0:1], made_send.at[k])

        @pl.when(edge == 0)
        def _():
            expect(made.at[k, 0:5], made_send.at[k])

        return carry

    lax.fori_loop(0, UNITS, drain, 0)

    def drain_out(q, carry):
        expect(sx.at[q], send.at[0, q])
        expect(rz.at[q], send.at[1, q])
        expect(sy.at[q], send.at[2, q])
        expect(rz.at[q], send.at[3, q])
        expect(rx.at[q], send.at[4, q])
        return carry

    lax.fori_loop(0, PARTS, drain_out, 0)


def sync_and_decode(grad, params, one, two, flat, combine):
    hbm = pl.BlockSpec(memory_space=pl.ANY)
    vmem = pl.BlockSpec(memory_space=pltpu.VMEM)
    block = (TILES, 8, 128)
    dma = pltpu.SemaphoreType.DMA
    return pl.pallas_call(
        kernel,
        out_shape=jax.ShapeDtypeStruct(flat.shape, BF),
        in_specs=[hbm] * 5 + [vmem],
        out_specs=vmem,
        scratch_shapes=[
            pltpu.VMEM((UNITS, EXPERTS, HELD, 8, WIDE), BF),
            pltpu.VMEM(params.shape, BF),
            pltpu.VMEM(one.shape, F32),
            pltpu.VMEM(two.shape, F32),
            pltpu.VMEM(flat.shape, BF),
            pltpu.VMEM((UNITS, 2 * NY) + block, BF),
            pltpu.VMEM((UNITS, NY) + block, BF),
            pltpu.VMEM((UNITS, NY) + block, BF),
            pltpu.VMEM((UNITS, NY) + block, BF),
            pltpu.VMEM((UNITS, 2 * NY) + block, BF),
            pltpu.VMEM((TILES * 64, 128), F32),
            pltpu.VMEM((3, TILES * 8, 128), F32),
            pltpu.VMEM(block, F32),
            pltpu.VMEM((HIDDEN, WIDE), BF),
            pltpu.VMEM((2, TOKENS, HIDDEN), F32),
            pltpu.VMEM((TOKENS, HIDDEN), BF),
            pltpu.VMEM((PARTS, TOKENS, WIDE), F32),
            pltpu.VMEM((PARTS, NX - 1, ROWS, WIDE), BF),
            pltpu.VMEM((PARTS, NX - 1, ROWS, WIDE), BF),
            pltpu.VMEM((PARTS, NZ, ROWS, 128), BF),
            pltpu.VMEM((PARTS, NZ - 1, ROWS, 128), BF),
            pltpu.VMEM((PARTS, ROWS, 128), BF),
            pltpu.VMEM((PARTS, ROWS, 128), BF),
            pltpu.VMEM((PARTS, NX, NZ, ROWS, 128), BF),
            dma((UNITS,)),
            dma((4,)),
            dma((UNITS,)),
            dma((UNITS,)),
            dma((UNITS,)),
            dma((UNITS, NY)),
            dma((UNITS, NY)),
            dma((UNITS,)),
            dma((UNITS, NY)),
            dma((UNITS,)),
            dma((UNITS,)),
            dma((5, PARTS)),
            dma((5, PARTS)),
        ],
        compiler_params=pltpu.CompilerParams(
            collective_id=0, has_side_effects=True, vmem_limit_bytes=63 * 2**20
        ),
    )(grad, params, one, two, flat, combine)


def shards(grad_partial, params, first_moment, second_moment, tokens, expert_ids, route_weights):
    steps, count, width = tokens.shape
    flat = tokens.reshape(steps * count, width)
    chosen = (expert_ids[..., None] == jnp.arange(EXPERTS, dtype=jnp.int32)).astype(F32)
    combine = jnp.sum(route_weights[..., None] * chosen, axis=-2).reshape(steps * count, EXPERTS)
    combine = jnp.repeat(combine, HIDDEN // EXPERTS, axis=1)
    grad = grad_partial[0].transpose(0, 1, 3, 2, 4)
    mixed = sync_and_decode(grad, params, first_moment, second_moment, flat, combine)
    return mixed.reshape(steps, count, width)


def solution(mesh):
    return jax.shard_map(
        shards,
        mesh=mesh,
        in_specs=(
            P("dp", None, None, None, "expert", None),
            P(None, None, ("dp", "expert"), None),
            P(None, None, ("dp", "expert"), None),
            P(None, None, ("dp", "expert"), None),
            P(None, "dp", None),
            P(None, "dp", None),
            P(None, "dp", None),
        ),
        out_specs=P(None, "dp", None),
        check_vma=False,
    )
```

```python
import jax
import jax.numpy as jnp
from jax import lax
from jax.experimental import pallas as pl
from jax.experimental.pallas import tpu as pltpu
from jax.sharding import PartitionSpec as P

D = 5120
EXPERTS = 3
HELD = 3
NY = 4
NX = 4
NZ = 8
ROWS = 16
WIDE = 1024
FOLD = WIDE // 128
PARTS = D // WIDE
UNITS = 3 * PARTS
TILES = EXPERTS * HELD
TOKENS = 64
HIDDEN = TILES * 8
RATE = 3.0 / D**0.5
MESH = pl.DeviceIdType.MESH
BF = jnp.bfloat16
F32 = jnp.float32


def remote(src, dst, send, recv, peer):
    return pltpu.make_async_remote_copy(
        src_ref=src, dst_ref=dst, send_sem=send, recv_sem=recv, device_id=peer, device_id_type=MESH
    )


def expect(ref, sem):
    pltpu.make_async_copy(ref, ref, sem).wait()


def kernel(
    grad_hbm,
    par_hbm,
    one_hbm,
    two_hbm,
    tok_hbm,
    ids_hbm,
    route_hbm,
    out_ref,
    gbuf,
    par,
    one,
    two,
    tok,
    ids,
    route,
    comb,
    fold,
    near,
    right,
    left,
    made,
    flat,
    opt,
    tot,
    wide,
    acc,
    hid,
    part,
    sx,
    rx,
    sz,
    rz,
    sy,
    ry,
    res,
    load_sem,
    in_sem,
    near_send,
    near_recv,
    line_send,
    right_recv,
    left_recv,
    made_send,
    made_recv,
    share_send,
    share_recv,
    send,
    recv,
):
    dp = lax.axis_index("dp")
    e = lax.axis_index("expert")
    y = dp // 2
    c = dp % 2
    half = e // (NX * NZ)
    z = (e // NX) % NZ
    x = e % NX
    x_peer = [(dp, half * NX * NZ + z * NX + (x + d) % NX) for d in range(1, NX)]
    z_peer = [(dp, half * NX * NZ + ((z + d) % NZ) * NX + x) for d in range(1, NZ)]
    far = (dp, (1 - half) * NX * NZ + z * NX + x)
    twin = (y * 2 + 1 - c, e)
    has_up = y < NY - 1
    has_down = y > 0
    edge = ((y == 0) | (y == NY - 1)).astype(jnp.int32)

    up = (((y + 1) % NY) * 2 + c, e)
    down = (((y + NY - 1) % NY) * 2 + c, e)
    peers = x_peer + z_peer + [far, twin, up, down]
    barrier = pltpu.get_barrier_semaphore()
    for peer in peers:
        pl.semaphore_signal(barrier, inc=1, device_id=peer, device_id_type=MESH)

    def lanes(q):
        return pl.ds(pl.multiple_of(q * WIDE, WIDE), WIDE)

    def load(k):
        return pltpu.make_async_copy(
            grad_hbm.at[:, k // PARTS, :, :, lanes(k % PARTS)], gbuf.at[k], load_sem.at[k]
        )

    inputs = [
        pltpu.make_async_copy(a, b, in_sem.at[i])
        for i, (a, b) in enumerate(
            (
                (ids_hbm, ids),
                (route_hbm, route),
                (par_hbm, par),
                (one_hbm, one),
                (two_hbm, two),
                (tok_hbm, tok),
            )
        )
    ]

    def start_load(k, carry):
        load(k).start()
        return carry

    lax.fori_loop(0, 2, start_load, 0)
    for copy in inputs:
        copy.start()
    lax.fori_loop(2, UNITS, start_load, 0)
    acc[...] = jnp.zeros_like(acc)

    def settle():
        for copy in inputs:
            copy.wait()
        member = lax.broadcasted_iota(jnp.int32, (8, HIDDEN), 1) // (HIDDEN // EXPERTS)
        member = (member == lax.broadcasted_iota(jnp.int32, (8, HIDDEN), 0)).astype(F32)
        steps, topk, count = ids.shape
        for s in range(steps):
            shares = []
            for g in range(EXPERTS):
                shares.append(jnp.sum(jnp.where(ids[s] == g, route[s], 0.0), axis=0, keepdims=True))
            shares.append(jnp.zeros((8 - EXPERTS, count), F32))
            comb[s * count : (s + 1) * count, :] = lax.dot_general(
                jnp.concatenate(shares, axis=0),
                member,
                (((0,), (0,)), ((), ())),
                precision=lax.Precision.HIGHEST,
                preferred_element_type=F32,
            )

    def cut(k):
        load(k).wait()

        def cut_group(g, carry):
            for j in range(HELD):
                v = gbuf[k, g, j].astype(F32)
                for s in range(FOLD):
                    flat[pl.ds(j * 64 + s, 8, stride=8), :] = v[:, s * 128 : (s + 1) * 128]
            for j in range(HELD):
                for b in range(8):
                    rows = flat[j * 64 + b * 8 : j * 64 + b * 8 + 8, :]
                    fold[k, (b % 2) * NY + b // 2, g * HELD + j] = rows.astype(BF)
            return carry

        lax.fori_loop(0, EXPERTS, cut_group, 0)

    def trade(k):
        remote(
            fold.at[k, pl.ds((1 - c) * NY, NY)], near.at[k], near_send.at[k], near_recv.at[k], twin
        ).start()

    def send_up(k, to):
        remote(
            fold.at[k, c * NY + to], right.at[k, to], line_send.at[k], right_recv.at[k, to], up
        ).start()

    def send_down(k, to):
        remote(
            fold.at[k, c * NY + to], left.at[k, to], line_send.at[k], left_recv.at[k, to], down
        ).start()

    def pair(k):
        expect(near.at[k], near_recv.at[k])

        def pair_one(i, carry):
            to = jnp.where(y < 2, NY - 1 - i, i)
            mine = c * NY + to
            fold[k, mine] = (fold[k, mine].astype(F32) + near[k, to].astype(F32)).astype(BF)

            @pl.when((y == 0) & (to > 0))
            def _():
                send_up(k, to)

            @pl.when((y == NY - 1) & (to < NY - 1))
            def _():
                send_down(k, to)

            return carry

        lax.fori_loop(0, NY, pair_one, 0)

    def pass_up(k):
        for to in (3, 2):

            @pl.when(to > y)
            def _():
                expect(right.at[k, to], right_recv.at[k, to])
                mine = c * NY + to
                fold[k, mine] = (fold[k, mine].astype(F32) + right[k, to].astype(F32)).astype(BF)
                send_up(k, to)

    def pass_down(k):
        for to in (0, 1):

            @pl.when(to < y)
            def _():
                expect(left.at[k, to], left_recv.at[k, to])
                mine = c * NY + to
                fold[k, mine] = (fold[k, mine].astype(F32) + left[k, to].astype(F32)).astype(BF)
                send_down(k, to)

    def share(k, of):
        remote(
            made.at[k, of * 2 + c], made.at[k, of * 2 + c], share_send.at[k], share_recv.at[k], twin
        ).start()

    def give_up(k, of):
        remote(
            made.at[k, of * 2 + c], made.at[k, of * 2 + c], made_send.at[k], made_recv.at[k, of], up
        ).start()

    def give_down(k, of):
        remote(
            made.at[k, of * 2 + c], made.at[k, of * 2 + c], made_send.at[k], made_recv.at[k, of], down
        ).start()

    def update(k):
        m = k // PARTS
        q = k % PARTS

        def place(g, carry):
            for i, source in enumerate((par, one, two)):
                v = source[g, m, :, lanes(q)].astype(F32)
                for s in range(FOLD):
                    opt[i, pl.ds(g * HELD * 8 + s, HELD, stride=8), :] = v[:, s * 128 : (s + 1) * 128]
            return carry

        lax.fori_loop(0, EXPERTS, place, 0)
        tot[...] = fold[k, c * NY + y].astype(F32)

        @pl.when(has_down)
        def _():
            expect(right.at[k, y], right_recv.at[k, y])
            tot[...] += right[k, y].astype(F32)

        @pl.when(has_up)
        def _():
            expect(left.at[k, y], left_recv.at[k, y])
            tot[...] += left[k, y].astype(F32)

        grad = tot[...].reshape(TILES * 8, 128)
        weights = opt[0]
        moment_one = 0.9 * opt[1] + 0.1 * grad
        moment_two = 0.95 * opt[2] + 0.05 * grad * grad
        step_dir = moment_one / (1.0 - 0.9**10) / (jnp.sqrt(moment_two / (1.0 - 0.95**10)) + 1e-08)
        fresh = weights - RATE * (step_dir + 0.1 * weights)
        made[k, dp] = fresh.reshape(TILES, 8, 128).astype(BF)

        @pl.when(has_up)
        def _():
            give_up(k, y)

        @pl.when(has_down)
        def _():
            give_down(k, y)

        share(k, y)

    def gather(k, of):
        expect(made.at[k, of * 2 + c], made_recv.at[k, of])

        @pl.when((of < y) & has_up)
        def _():
            give_up(k, of)

        @pl.when((of > y) & has_down)
        def _():
            give_down(k, of)

        share(k, of)

    def apply(k):
        m = k // PARTS
        q = k % PARTS
        expect(near.at[k], share_recv.at[k])

        def spread(t, carry):
            base = pl.multiple_of(t * 64, 64)
            for b in range(8):
                flat[pl.ds(base + b * 8, 8), :] = made[k, b, t].astype(F32)
            return carry

        def weave(s, carry):
            rows = [flat[pl.ds(t * 64 + s, 8, stride=8), :] for t in range(TILES)]
            columns = pl.ds(pl.multiple_of(s * 128, 128), 128)
            wide[:, columns] = jnp.concatenate(rows, axis=0).astype(BF)
            return carry

        lax.fori_loop(0, TILES, spread, 0)
        lax.fori_loop(0, FOLD, weave, 0)

        @pl.when(m < 2)
        def _():
            acc[m] += lax.dot_general(
                tok[:, lanes(q)], wide[...], (((1,), (1,)), ((), ())), preferred_element_type=F32
            )

        @pl.when(k == 2 * PARTS - 1)
        def _():
            gate = acc[0]
            hid[...] = (comb[...] * (gate / (1.0 + jnp.exp(-gate))) * acc[1]).astype(BF)

        @pl.when(m == 2)
        def _():
            part[q] = jnp.dot(hid[...], wide[...], preferred_element_type=F32)
            for d in range(1, NX):
                to = (x + d) % NX
                rows = pl.ds(pl.multiple_of(to * ROWS, ROWS), ROWS)
                sx[q, d - 1] = part[q, rows, :].astype(BF)
                remote(sx.at[q, d - 1], rx.at[q, d - 1], send.at[0, q], recv.at[0, q], x_peer[d - 1]).start()

    def z_out(q):
        expect(rx.at[q], recv.at[0, q])
        rows = pl.ds(pl.multiple_of(x * ROWS, ROWS), ROWS)
        total = part[q, rows, :]
        for d in range(1, NX):
            total += rx[q, d - 1].astype(F32)
        total = total.astype(BF)
        for k in range(NZ):
            sz[q, k] = total[:, k * 128 : (k + 1) * 128]

        def one_z(d, carry):
            to = (z + d) % NZ
            peer = (dp, half * NX * NZ + to * NX + x)
            remote(sz.at[q, to], rz.at[q, d - 1], send.at[1, q], recv.at[1, q], peer).start()
            return carry

        lax.fori_loop(1, NZ, one_z, 0)

    def y_out(q):
        expect(rz.at[q], recv.at[1, q])
        total = sz[q, z].astype(F32)
        for d in range(1, NZ):
            total += rz[q, d - 1].astype(F32)
        sy[q] = total.astype(BF)
        remote(sy.at[q], ry.at[q], send.at[2, q], recv.at[2, q], far).start()

    def z_back(q):
        expect(ry.at[q], recv.at[2, q])
        total = sy[q].astype(F32) + ry[q].astype(F32)
        res[q, x, z] = total.astype(BF)

        def one_z(d, carry):
            peer = (dp, half * NX * NZ + ((z + d) % NZ) * NX + x)
            remote(res.at[q, x, z], res.at[q, x, z], send.at[3, q], recv.at[3, q], peer).start()
            return carry

        lax.fori_loop(1, NZ, one_z, 0)

    def x_back(q):
        expect(rz.at[q], recv.at[3, q])
        for d in range(1, NX):
            remote(res.at[q, x], res.at[q, x], send.at[4, q], recv.at[4, q], x_peer[d - 1]).start()

    def finish(q):
        expect(rx.at[q], recv.at[4, q])

        def put(k, carry):
            columns = pl.ds(pl.multiple_of(q * WIDE + k * 128, 128), 128)
            for i in range(NX):
                out_ref[i * ROWS : (i + 1) * ROWS, columns] = res[q, i, k]
            return carry

        lax.fori_loop(0, NZ, put, 0)

    def turn(i, carry):
        def at(lag, stage, also=None, first=0):
            k = i - lag
            ok = (k >= first) & (k < UNITS)
            if also is not None:
                ok = ok & also

            @pl.when(ok)
            def _():
                stage(k)

        pl.when(i == 1)(settle)
        middle = edge == 0
        at(0, trade)
        at(1, pair)
        at(1 + 2 * y, pass_up, middle)
        at(1 + 2 * (3 - y), pass_down, middle)
        at(1 + 2 * (2 + edge), update)

        def look(j, carry):
            far_off = 1 + j // 2
            of = jnp.where(j % 2 == 0, y - far_off, y + far_off)
            made_at = 1 + 2 * (2 + ((of == 0) | (of == NY - 1)).astype(jnp.int32))
            at(made_at + 2 * far_off, lambda k: gather(k, of), (of >= 0) & (of < NY))
            return carry

        lax.fori_loop(0, 2 * (NY - 1), look, 0)
        done = 2 + 10 + 2 * edge
        at(done, apply)
        for lag, stage in zip((2, 4, 7, 10, 12), (z_out, y_out, z_back, x_back, finish)):
            at(done + lag, lambda k, stage=stage: stage(k - 2 * PARTS), None, 2 * PARTS)
        at(-1, cut)
        return carry

    cut(0)
    pl.semaphore_wait(barrier, len(peers))
    lax.fori_loop(0, UNITS + 26, turn, 0)

    def drain(k, carry):
        expect(near.at[k], near_send.at[k])
        expect(near.at[k, 0:3], line_send.at[k])
        expect(near.at[k], share_send.at[k])

        @pl.when(edge == 1)
        def _():
            expect(made.at[k, 0:1], made_send.at[k])

        @pl.when(edge == 0)
        def _():
            expect(made.at[k, 0:5], made_send.at[k])

        return carry

    lax.fori_loop(0, UNITS, drain, 0)

    def drain_out(q, carry):
        expect(sx.at[q], send.at[0, q])
        expect(rz.at[q], send.at[1, q])
        expect(sy.at[q], send.at[2, q])
        expect(rz.at[q], send.at[3, q])
        expect(rx.at[q], send.at[4, q])
        return carry

    lax.fori_loop(0, PARTS, drain_out, 0)


def sync_and_decode(grad, params, one, two, flat, ids, route):
    hbm = pl.BlockSpec(memory_space=pl.ANY)
    vmem = pl.BlockSpec(memory_space=pltpu.VMEM)
    block = (TILES, 8, 128)
    dma = pltpu.SemaphoreType.DMA
    return pl.pallas_call(
        kernel,
        out_shape=jax.ShapeDtypeStruct(flat.shape, BF),
        in_specs=[hbm] * 7,
        out_specs=vmem,
        scratch_shapes=[
            pltpu.VMEM((UNITS, EXPERTS, HELD, 8, WIDE), BF),
            pltpu.VMEM(params.shape, BF),
            pltpu.VMEM(one.shape, F32),
            pltpu.VMEM(two.shape, F32),
            pltpu.VMEM(flat.shape, BF),
            pltpu.VMEM(ids.shape, jnp.int32),
            pltpu.VMEM(route.shape, F32),
            pltpu.VMEM((TOKENS, HIDDEN), F32),
            pltpu.VMEM((UNITS, 2 * NY) + block, BF),
            pltpu.VMEM((UNITS, NY) + block, BF),
            pltpu.VMEM((UNITS, NY) + block, BF),
            pltpu.VMEM((UNITS, NY) + block, BF),
            pltpu.VMEM((UNITS, 2 * NY) + block, BF),
            pltpu.VMEM((TILES * 64, 128), F32),
            pltpu.VMEM((3, TILES * 8, 128), F32),
            pltpu.VMEM(block, F32),
            pltpu.VMEM((HIDDEN, WIDE), BF),
            pltpu.VMEM((2, TOKENS, HIDDEN), F32),
            pltpu.VMEM((TOKENS, HIDDEN), BF),
            pltpu.VMEM((PARTS, TOKENS, WIDE), F32),
            pltpu.VMEM((PARTS, NX - 1, ROWS, WIDE), BF),
            pltpu.VMEM((PARTS, NX - 1, ROWS, WIDE), BF),
            pltpu.VMEM((PARTS, NZ, ROWS, 128), BF),
            pltpu.VMEM((PARTS, NZ - 1, ROWS, 128), BF),
            pltpu.VMEM((PARTS, ROWS, 128), BF),
            pltpu.VMEM((PARTS, ROWS, 128), BF),
            pltpu.VMEM((PARTS, NX, NZ, ROWS, 128), BF),
            dma((UNITS,)),
            dma((6,)),
            dma((UNITS,)),
            dma((UNITS,)),
            dma((UNITS,)),
            dma((UNITS, NY)),
            dma((UNITS, NY)),
            dma((UNITS,)),
            dma((UNITS, NY)),
            dma((UNITS,)),
            dma((UNITS,)),
            dma((5, PARTS)),
            dma((5, PARTS)),
        ],
        compiler_params=pltpu.CompilerParams(
            collective_id=0, has_side_effects=True, vmem_limit_bytes=63 * 2**20
        ),
    )(grad, params, one, two, flat, ids, route)


def shards(grad_partial, params, first_moment, second_moment, tokens, expert_ids, route_weights):
    steps, count, width = tokens.shape
    flat = tokens.reshape(steps * count, width)
    grad = grad_partial[0].transpose(0, 1, 3, 2, 4)
    mixed = sync_and_decode(grad, params, first_moment, second_moment, flat, expert_ids.transpose(0, 2, 1), route_weights.transpose(0, 2, 1))
    return mixed.reshape(steps, count, width)


def solution(mesh):
    return jax.shard_map(
        shards,
        mesh=mesh,
        in_specs=(
            P("dp", None, None, None, "expert", None),
            P(None, None, ("dp", "expert"), None),
            P(None, None, ("dp", "expert"), None),
            P(None, None, ("dp", "expert"), None),
            P(None, "dp", None),
            P(None, "dp", None),
            P(None, "dp", None),
        ),
        out_specs=P(None, "dp", None),
        check_vma=False,
    )
```

```python
import jax
import jax.numpy as jnp
from jax import lax
from jax.experimental import pallas as pl
from jax.experimental.pallas import tpu as pltpu
from jax.sharding import PartitionSpec as P

D = 5120
EXPERTS = 3
HELD = 3
NY = 4
NX = 4
NZ = 8
ROWS = 16
WIDE = 1024
FOLD = WIDE // 128
PARTS = D // WIDE
UNITS = 3 * PARTS
TILES = EXPERTS * HELD
TOKENS = 64
HIDDEN = TILES * 8
RATE = 3.0 / D**0.5
MESH = pl.DeviceIdType.MESH
BF = jnp.bfloat16
F32 = jnp.float32


def remote(src, dst, send, recv, peer):
    return pltpu.make_async_remote_copy(
        src_ref=src, dst_ref=dst, send_sem=send, recv_sem=recv, device_id=peer, device_id_type=MESH
    )


def expect(ref, sem):
    pltpu.make_async_copy(ref, ref, sem).wait()


def kernel(
    grad_hbm,
    par_hbm,
    one_hbm,
    two_hbm,
    tok_hbm,
    ids_hbm,
    route_hbm,
    out_ref,
    gbuf,
    par,
    one,
    two,
    tok,
    ids,
    route,
    comb,
    fold,
    near,
    right,
    left,
    made,
    flat,
    opt,
    tot,
    wide,
    acc,
    hid,
    part,
    sx,
    rx,
    sz,
    rz,
    sy,
    ry,
    res,
    load_sem,
    in_sem,
    near_send,
    near_recv,
    line_send,
    right_recv,
    left_recv,
    made_send,
    made_recv,
    share_send,
    share_recv,
    send,
    recv,
):
    dp = lax.axis_index("dp")
    e = lax.axis_index("expert")
    y = dp // 2
    c = dp % 2
    half = e // (NX * NZ)
    z = (e // NX) % NZ
    x = e % NX
    x_peer = [(dp, half * NX * NZ + z * NX + (x + d) % NX) for d in range(1, NX)]
    z_peer = [(dp, half * NX * NZ + ((z + d) % NZ) * NX + x) for d in range(1, NZ)]
    far = (dp, (1 - half) * NX * NZ + z * NX + x)
    twin = (y * 2 + 1 - c, e)
    has_up = y < NY - 1
    has_down = y > 0
    edge = ((y == 0) | (y == NY - 1)).astype(jnp.int32)

    up = (((y + 1) % NY) * 2 + c, e)
    down = (((y + NY - 1) % NY) * 2 + c, e)
    peers = x_peer + z_peer + [far, twin, up, down]
    barrier = pltpu.get_barrier_semaphore()
    for peer in peers:
        pl.semaphore_signal(barrier, inc=1, device_id=peer, device_id_type=MESH)

    def lanes(q):
        return pl.ds(pl.multiple_of(q * WIDE, WIDE), WIDE)

    def load(k):
        return pltpu.make_async_copy(
            grad_hbm.at[:, k // PARTS, :, :, lanes(k % PARTS)], gbuf.at[k], load_sem.at[k]
        )

    inputs = [
        pltpu.make_async_copy(a, b, in_sem.at[i])
        for i, (a, b) in enumerate(
            (
                (ids_hbm, ids),
                (route_hbm, route),
                (par_hbm, par),
                (one_hbm, one),
                (two_hbm, two),
                (tok_hbm, tok),
            )
        )
    ]

    def start_load(k, carry):
        load(k).start()
        return carry

    lax.fori_loop(0, 2, start_load, 0)
    for copy in inputs:
        copy.start()
    lax.fori_loop(2, UNITS, start_load, 0)
    acc[...] = jnp.zeros_like(acc)

    def settle():
        for copy in inputs:
            copy.wait()
        member = lax.broadcasted_iota(jnp.int32, (8, HIDDEN), 1) // (HIDDEN // EXPERTS)
        member = (member == lax.broadcasted_iota(jnp.int32, (8, HIDDEN), 0)).astype(F32)
        steps, topk, count = ids.shape
        for s in range(steps):
            shares = []
            for g in range(EXPERTS):
                shares.append(jnp.sum(jnp.where(ids[s] == g, route[s], 0.0), axis=0, keepdims=True))
            shares.append(jnp.zeros((8 - EXPERTS, count), F32))
            comb[s * count : (s + 1) * count, :] = lax.dot_general(
                jnp.concatenate(shares, axis=0),
                member,
                (((0,), (0,)), ((), ())),
                precision=lax.Precision.HIGHEST,
                preferred_element_type=F32,
            )

    def cut(k):
        load(k).wait()

        def cut_group(g, carry):
            for j in range(HELD):
                v = gbuf[k, g, j].astype(F32)
                for s in range(FOLD):
                    flat[pl.ds(j * 64 + s, 8, stride=8), :] = v[:, s * 128 : (s + 1) * 128]
            for j in range(HELD):
                for b in range(8):
                    rows = flat[j * 64 + b * 8 : j * 64 + b * 8 + 8, :]
                    fold[k, (b % 2) * NY + b // 2, g * HELD + j] = rows.astype(BF)
            return carry

        lax.fori_loop(0, EXPERTS, cut_group, 0)

    def trade(k):
        remote(
            fold.at[k, pl.ds((1 - c) * NY, NY)], near.at[k], near_send.at[k], near_recv.at[k], twin
        ).start()

    def send_up(k, to):
        remote(
            fold.at[k, c * NY + to], right.at[k, to], line_send.at[k], right_recv.at[k, to], up
        ).start()

    def send_down(k, to):
        remote(
            fold.at[k, c * NY + to], left.at[k, to], line_send.at[k], left_recv.at[k, to], down
        ).start()

    def pair(k):
        expect(near.at[k], near_recv.at[k])

        def pair_one(i, carry):
            to = jnp.where(y < 2, NY - 1 - i, i)
            mine = c * NY + to
            fold[k, mine] = (fold[k, mine].astype(F32) + near[k, to].astype(F32)).astype(BF)

            @pl.when((y == 0) & (to > 0))
            def _():
                send_up(k, to)

            @pl.when((y == NY - 1) & (to < NY - 1))
            def _():
                send_down(k, to)

            return carry

        lax.fori_loop(0, NY, pair_one, 0)

    def pass_up(k):
        for to in (3, 2):

            @pl.when(to > y)
            def _():
                expect(right.at[k, to], right_recv.at[k, to])
                mine = c * NY + to
                fold[k, mine] = (fold[k, mine].astype(F32) + right[k, to].astype(F32)).astype(BF)
                send_up(k, to)

    def pass_down(k):
        for to in (0, 1):

            @pl.when(to < y)
            def _():
                expect(left.at[k, to], left_recv.at[k, to])
                mine = c * NY + to
                fold[k, mine] = (fold[k, mine].astype(F32) + left[k, to].astype(F32)).astype(BF)
                send_down(k, to)

    def share(k, of):
        remote(
            made.at[k, of * 2 + c], made.at[k, of * 2 + c], share_send.at[k], share_recv.at[k], twin
        ).start()

    def give_up(k, of):
        remote(
            made.at[k, of * 2 + c], made.at[k, of * 2 + c], made_send.at[k], made_recv.at[k, of], up
        ).start()

    def give_down(k, of):
        remote(
            made.at[k, of * 2 + c], made.at[k, of * 2 + c], made_send.at[k], made_recv.at[k, of], down
        ).start()

    def update(k):
        m = k // PARTS
        q = k % PARTS

        def place(g, carry):
            for i, source in enumerate((par, one, two)):
                v = source[g, m, :, lanes(q)].astype(F32)
                for s in range(FOLD):
                    opt[i, pl.ds(g * HELD * 8 + s, HELD, stride=8), :] = v[:, s * 128 : (s + 1) * 128]
            return carry

        lax.fori_loop(0, EXPERTS, place, 0)
        tot[...] = fold[k, c * NY + y].astype(F32)

        @pl.when(has_down)
        def _():
            expect(right.at[k, y], right_recv.at[k, y])
            tot[...] += right[k, y].astype(F32)

        @pl.when(has_up)
        def _():
            expect(left.at[k, y], left_recv.at[k, y])
            tot[...] += left[k, y].astype(F32)

        grad = tot[...].reshape(TILES * 8, 128)
        weights = opt[0]
        moment_one = 0.9 * opt[1] + 0.1 * grad
        moment_two = 0.95 * opt[2] + 0.05 * grad * grad
        step_dir = moment_one / (1.0 - 0.9**10) / (jnp.sqrt(moment_two / (1.0 - 0.95**10)) + 1e-08)
        fresh = weights - RATE * (step_dir + 0.1 * weights)
        made[k, dp] = fresh.reshape(TILES, 8, 128).astype(BF)

        @pl.when(has_up)
        def _():
            give_up(k, y)

        @pl.when(has_down)
        def _():
            give_down(k, y)

        share(k, y)

    def gather(k, of):
        expect(made.at[k, of * 2 + c], made_recv.at[k, of])

        @pl.when((of < y) & has_up)
        def _():
            give_up(k, of)

        @pl.when((of > y) & has_down)
        def _():
            give_down(k, of)

        share(k, of)

    def apply(k):
        m = k // PARTS
        q = k % PARTS
        expect(near.at[k], share_recv.at[k])

        def spread(t, carry):
            base = pl.multiple_of(t * 64, 64)
            for b in range(8):
                flat[pl.ds(base + b * 8, 8), :] = made[k, b, t].astype(F32)
            return carry

        def weave(s, carry):
            rows = [flat[pl.ds(t * 64 + s, 8, stride=8), :] for t in range(TILES)]
            columns = pl.ds(pl.multiple_of(s * 128, 128), 128)
            wide[:, columns] = jnp.concatenate(rows, axis=0).astype(BF)
            return carry

        lax.fori_loop(0, TILES, spread, 0)
        lax.fori_loop(0, FOLD, weave, 0)

        @pl.when(m < 2)
        def _():
            acc[m] += lax.dot_general(
                tok[:, lanes(q)], wide[...], (((1,), (1,)), ((), ())), preferred_element_type=F32
            )

        @pl.when(k == 2 * PARTS - 1)
        def _():
            gate = acc[0]
            hid[...] = (comb[...] * (gate / (1.0 + jnp.exp(-gate))) * acc[1]).astype(BF)

        @pl.when(m == 2)
        def _():
            part[q] = jnp.dot(hid[...], wide[...], preferred_element_type=F32)
            for d in range(1, NX):
                to = (x + d) % NX
                rows = pl.ds(pl.multiple_of(to * ROWS, ROWS), ROWS)
                sx[q, d - 1] = part[q, rows, :].astype(BF)
                remote(sx.at[q, d - 1], rx.at[q, d - 1], send.at[0, q], recv.at[0, q], x_peer[d - 1]).start()

    def z_out(q):
        expect(rx.at[q], recv.at[0, q])
        rows = pl.ds(pl.multiple_of(x * ROWS, ROWS), ROWS)
        total = part[q, rows, :]
        for d in range(1, NX):
            total += rx[q, d - 1].astype(F32)
        total = total.astype(BF)
        for k in range(NZ):
            sz[q, k] = total[:, k * 128 : (k + 1) * 128]

        def one_z(d, carry):
            to = (z + d) % NZ
            peer = (dp, half * NX * NZ + to * NX + x)
            remote(sz.at[q, to], rz.at[q, d - 1], send.at[1, q], recv.at[1, q], peer).start()
            return carry

        lax.fori_loop(1, NZ, one_z, 0)

    def y_out(q):
        expect(rz.at[q], recv.at[1, q])
        total = sz[q, z].astype(F32)
        for d in range(1, NZ):
            total += rz[q, d - 1].astype(F32)
        sy[q] = total.astype(BF)
        remote(sy.at[q], ry.at[q], send.at[2, q], recv.at[2, q], far).start()

    def z_back(q):
        expect(ry.at[q], recv.at[2, q])
        total = sy[q].astype(F32) + ry[q].astype(F32)
        res[q, x, z] = total.astype(BF)

        def one_z(d, carry):
            peer = (dp, half * NX * NZ + ((z + d) % NZ) * NX + x)
            remote(res.at[q, x, z], res.at[q, x, z], send.at[3, q], recv.at[3, q], peer).start()
            return carry

        lax.fori_loop(1, NZ, one_z, 0)

    def x_back(q):
        expect(rz.at[q], recv.at[3, q])
        for d in range(1, NX):
            remote(res.at[q, x], res.at[q, x], send.at[4, q], recv.at[4, q], x_peer[d - 1]).start()

    def finish(q):
        expect(rx.at[q], recv.at[4, q])

        def put(k, carry):
            columns = pl.ds(pl.multiple_of(q * WIDE + k * 128, 128), 128)
            for i in range(NX):
                out_ref[i * ROWS : (i + 1) * ROWS, columns] = res[q, i, k]
            return carry

        lax.fori_loop(0, NZ, put, 0)
        drain_out(q)

    def drain(k):
        expect(near.at[k], near_send.at[k])
        expect(near.at[k, 0:3], line_send.at[k])
        expect(near.at[k], share_send.at[k])

        @pl.when(edge == 1)
        def _():
            expect(made.at[k, 0:1], made_send.at[k])

        @pl.when(edge == 0)
        def _():
            expect(made.at[k, 0:5], made_send.at[k])

    def drain_out(q):
        expect(sx.at[q], send.at[0, q])
        expect(rz.at[q], send.at[1, q])
        expect(sy.at[q], send.at[2, q])
        expect(rz.at[q], send.at[3, q])
        expect(rx.at[q], send.at[4, q])

    def turn(i, carry):
        def at(lag, stage, also=None, first=0):
            k = i - lag
            ok = (k >= first) & (k < UNITS)
            if also is not None:
                ok = ok & also

            @pl.when(ok)
            def _():
                stage(k)

        pl.when(i == 1)(settle)
        middle = edge == 0
        at(0, trade)
        at(1, pair)
        at(1 + 2 * y, pass_up, middle)
        at(1 + 2 * (3 - y), pass_down, middle)
        at(1 + 2 * (2 + edge), update)

        def look(j, carry):
            far_off = 1 + j // 2
            of = jnp.where(j % 2 == 0, y - far_off, y + far_off)
            made_at = 1 + 2 * (2 + ((of == 0) | (of == NY - 1)).astype(jnp.int32))
            at(made_at + 2 * far_off, lambda k: gather(k, of), (of >= 0) & (of < NY))
            return carry

        lax.fori_loop(0, 2 * (NY - 1), look, 0)
        done = 2 + 10 + 2 * edge
        at(done, apply)
        for lag, stage in zip((3, 6, 9, 12, 14), (z_out, y_out, z_back, x_back, finish)):
            at(done + lag, lambda k, stage=stage: stage(k - 2 * PARTS), None, 2 * PARTS)
        at(done + 2, drain)
        at(-1, cut)
        return carry

    cut(0)
    pl.semaphore_wait(barrier, len(peers))
    lax.fori_loop(0, UNITS + 28, turn, 0)


def sync_and_decode(grad, params, one, two, flat, ids, route):
    hbm = pl.BlockSpec(memory_space=pl.ANY)
    vmem = pl.BlockSpec(memory_space=pltpu.VMEM)
    block = (TILES, 8, 128)
    dma = pltpu.SemaphoreType.DMA
    return pl.pallas_call(
        kernel,
        out_shape=jax.ShapeDtypeStruct(flat.shape, BF),
        in_specs=[hbm] * 7,
        out_specs=vmem,
        scratch_shapes=[
            pltpu.VMEM((UNITS, EXPERTS, HELD, 8, WIDE), BF),
            pltpu.VMEM(params.shape, BF),
            pltpu.VMEM(one.shape, F32),
            pltpu.VMEM(two.shape, F32),
            pltpu.VMEM(flat.shape, BF),
            pltpu.VMEM(ids.shape, jnp.int32),
            pltpu.VMEM(route.shape, F32),
            pltpu.VMEM((TOKENS, HIDDEN), F32),
            pltpu.VMEM((UNITS, 2 * NY) + block, BF),
            pltpu.VMEM((UNITS, NY) + block, BF),
            pltpu.VMEM((UNITS, NY) + block, BF),
            pltpu.VMEM((UNITS, NY) + block, BF),
            pltpu.VMEM((UNITS, 2 * NY) + block, BF),
            pltpu.VMEM((TILES * 64, 128), F32),
            pltpu.VMEM((3, TILES * 8, 128), F32),
            pltpu.VMEM(block, F32),
            pltpu.VMEM((HIDDEN, WIDE), BF),
            pltpu.VMEM((2, TOKENS, HIDDEN), F32),
            pltpu.VMEM((TOKENS, HIDDEN), BF),
            pltpu.VMEM((PARTS, TOKENS, WIDE), F32),
            pltpu.VMEM((PARTS, NX - 1, ROWS, WIDE), BF),
            pltpu.VMEM((PARTS, NX - 1, ROWS, WIDE), BF),
            pltpu.VMEM((PARTS, NZ, ROWS, 128), BF),
            pltpu.VMEM((PARTS, NZ - 1, ROWS, 128), BF),
            pltpu.VMEM((PARTS, ROWS, 128), BF),
            pltpu.VMEM((PARTS, ROWS, 128), BF),
            pltpu.VMEM((PARTS, NX, NZ, ROWS, 128), BF),
            dma((UNITS,)),
            dma((6,)),
            dma((UNITS,)),
            dma((UNITS,)),
            dma((UNITS,)),
            dma((UNITS, NY)),
            dma((UNITS, NY)),
            dma((UNITS,)),
            dma((UNITS, NY)),
            dma((UNITS,)),
            dma((UNITS,)),
            dma((5, PARTS)),
            dma((5, PARTS)),
        ],
        compiler_params=pltpu.CompilerParams(
            collective_id=0, has_side_effects=True, vmem_limit_bytes=63 * 2**20
        ),
    )(grad, params, one, two, flat, ids, route)


def shards(grad_partial, params, first_moment, second_moment, tokens, expert_ids, route_weights):
    steps, count, width = tokens.shape
    flat = tokens.reshape(steps * count, width)
    grad = grad_partial[0].transpose(0, 1, 3, 2, 4)
    mixed = sync_and_decode(grad, params, first_moment, second_moment, flat, expert_ids.transpose(0, 2, 1), route_weights.transpose(0, 2, 1))
    return mixed.reshape(steps, count, width)


def solution(mesh):
    return jax.shard_map(
        shards,
        mesh=mesh,
        in_specs=(
            P("dp", None, None, None, "expert", None),
            P(None, None, ("dp", "expert"), None),
            P(None, None, ("dp", "expert"), None),
            P(None, None, ("dp", "expert"), None),
            P(None, "dp", None),
            P(None, "dp", None),
            P(None, "dp", None),
        ),
        out_specs=P(None, "dp", None),
        check_vma=False,
    )
```
